32 devices in a mesh: chan: 4 (over x, core), blk: 8 (over z, y).
Axes of the slice: x: 2, y: 2, z: 4, core: 2. Of those that a mesh axis runs over, the one named last changes fastest.
Arguments:
- t_matrix: bfloat16 [4, 1024, 1024], P('chan', 'blk'), may hold values from -0.1875 to 0.1875
- v_jacobi: bfloat16 [4, 1024, 1024], P('chan'), may hold values from -6 to 6
- channel_dims: int32 [4], P('chan'), may hold values from 128 to 1024, as said below
- owner_map: int32 [4], replicated, may hold values from 0 to 3, each once
Outputs:
- triplet_blocks: bfloat16 [4, 4, 1024, 256], P('chan', None, 'blk')
The draws below stay inside these ranges and needn't reach their ends.
Inputs may be any that keep to these rules, and one draw needn't show every extreme that they name: `channel_dims`: channel 0 has exactly 1024 live states; others vary.
All inputs are finite; a program needn't handle non-finite values.
Results may differ from the reference program's by a relative error of at most 0.0058.
Values may be sent and summed in bfloat16 or wider, within the bound.
No kernel may reach another device: no remote copies, remote signals or barrier semaphores. Data moves between devices by JAX's collectives and lax.ppermute only.
A program may use at most 64 MiB of HBM per device.

```python
import jax
import jax.numpy as jnp
from jax import lax

NJ = 1024
CHANNELS = 4
NL = 1024
CB = 256
N_CHAN = 4


def draw_channel_dims(key, part):
    drawn = jax.random.randint(key, (CHANNELS,), NJ // 8, NJ + 1).astype(jnp.int32)
    return drawn.at[0].set(NJ)


def level_of(rng, extent, shards, low, top_value):
    def one(axis_at, shards_of):
        steps = jax.random.uniform(jax.random.fold_in(jax.random.fold_in(rng, 6), axis_at), (shards_of,), jnp.float32, low / len(shards), top_value / len(shards))
        return jnp.repeat(jnp.exp(steps), extent[axis_at] // shards_of).reshape((-1,) + (1,) * (len(extent) - axis_at - 1))

    level = one(*shards[0])
    for cut in shards[1:]:
        level = level * one(*cut)
    return level


def gaussian(stream_key, extent, width, bound, cuts=(), held_as=jnp.bfloat16):
    values = width * jax.random.normal(stream_key, extent, jnp.float32)
    if cuts:
        values = values * level_of(stream_key, extent, cuts, -0.22, 0.18)
    return jnp.clip(values, -bound, bound).astype(held_as)


def setup_inputs(seed: int = 0) -> dict:
    key_list = jax.random.split(jax.random.key(seed), 5)
    t_matrix = gaussian(key_list[0], (CHANNELS, NL, NJ), NJ ** -0.5, 0.1875, ((0, 4), (1, 8)))
    v_jacobi = gaussian(key_list[1], (CHANNELS, NJ, NJ), 1.0, 6.0, ((0, 4),))
    channel_dims = draw_channel_dims(jax.random.fold_in(key_list[4], 71), 0)
    owner_map = jax.random.permutation(key_list[3], N_CHAN).astype(jnp.int32)
    return {"t_matrix": t_matrix, "v_jacobi": v_jacobi, "channel_dims": channel_dims, "owner_map": owner_map}


def one_channel(packed):
    t_rows, v_raw, live = packed
    positions = jnp.arange(NJ, dtype=jnp.int32)
    kept_mask = (positions < live).astype(jnp.float32)
    v_float = v_raw.astype(jnp.float32)
    v_masked = ((v_float + v_float.T) * 0.5 * kept_mask[:, None] * kept_mask[None, :]).astype(jnp.bfloat16)
    weighted = jnp.dot(t_rows, v_masked, preferred_element_type=jnp.float32).astype(jnp.bfloat16)
    return jnp.dot(weighted, t_rows.T, preferred_element_type=jnp.float32).astype(jnp.bfloat16)


def reference(t_matrix, v_jacobi, channel_dims, owner_map):
    lab_rows = lax.map(one_channel, (t_matrix, v_jacobi, channel_dims))
    owners = jnp.arange(N_CHAN, dtype=jnp.int32)
    source_block = jnp.sum(owners[None, :] * (owner_map[None, :] == owners[:, None]).astype(jnp.int32), axis=1).astype(jnp.int32)
    col_blocks = lab_rows.reshape(CHANNELS, NL, N_CHAN, CB)
    picked = jnp.take(col_blocks, source_block, axis=2)
    return jnp.transpose(picked, (2, 0, 1, 3))
```

```python
import functools

import jax
import jax.numpy as jnp
import numpy as np
from jax import lax
from jax.experimental import pallas as pl
from jax.experimental.pallas import tpu as pltpu
from jax.sharding import Mesh, PartitionSpec as P

F32 = jnp.float32
BF16 = jnp.bfloat16
VMEM_LIMIT = 48 * 1024 * 1024


def dot_nt(a, b):
    return lax.dot_general(a, b, (((1,), (1,)), ((), ())), preferred_element_type=F32)


def weights_kernel(live_ref, v_ref, *refs):
    n_rows = (len(refs) - 1) // 2
    t_refs, vm_ref, w_refs = refs[:n_rows], refs[n_rows], refs[n_rows + 1 :]
    width = v_ref.shape[0]
    tile = min(256, width)
    live = live_ref[0]
    for i in range(0, width, tile):
        row_live = lax.broadcasted_iota(jnp.int32, (tile, tile), 0) + i < live
        for j in range(0, width, tile):
            col_live = lax.broadcasted_iota(jnp.int32, (tile, tile), 1) + j < live
            here = v_ref[i : i + tile, j : j + tile].astype(F32)
            there = v_ref[j : j + tile, i : i + tile].astype(F32)
            mean = (here + there.T) * 0.5
            vm_ref[i : i + tile, j : j + tile] = jnp.where(row_live & col_live, mean, 0.0).astype(BF16)
    for t_ref, w_ref in zip(t_refs, w_refs):
        w_ref[...] = jnp.dot(t_ref[...], vm_ref[...], preferred_element_type=F32).astype(BF16)


def tiles_kernel(n_w, n_t, n_half, half, place_ref, *refs):
    w_refs, t_refs = refs[:n_w], refs[n_w : n_w + n_t]
    vm_ref = refs[n_w + n_t]
    h_refs = refs[n_w + n_t + 1 : n_w + n_t + 1 + n_half]
    out_ref, shares, picked = refs[n_w + n_t + 1 + n_half :]
    groups = n_half
    rows = w_refs[0].shape[0]
    for k, h_ref in enumerate(h_refs):
        shares[k] = h_ref[...]
    for d in range(groups):
        picked[d * half : (d + 1) * half, :] = shares[place_ref[d]]
    first = lax.broadcasted_iota(jnp.int32, (rows // 2, 2 * half), 1) < half
    for k in range(n_w + n_t):
        if k < n_w:
            left = w_refs[k][...]
        else:
            left = jnp.dot(t_refs[k - n_w][...], vm_ref[...], preferred_element_type=F32).astype(BF16)
        place = place_ref[groups + k]
        for pair in range(groups // 2):
            both = dot_nt(left, picked[pair * 2 * half : (pair + 1) * 2 * half, :])
            top, bottom = both[: rows // 2], both[rows // 2 :]
            even = jnp.where(first, top, pltpu.roll(bottom, half, 1))
            odd = jnp.where(first, pltpu.roll(top, half, 1), bottom)
            out_ref[2 * pair, place] = even.astype(BF16)
            out_ref[2 * pair + 1, place] = odd.astype(BF16)


def place_kernel(ny, half, swap_ref, in_ref, out_ref):
    channels = in_ref.shape[0]
    deep = in_ref.shape[2]
    first = lax.broadcasted_iota(jnp.int32, (deep, 2 * half), 1) < half
    swap = swap_ref[0] > 0
    for c in range(channels):
        for y in range(ny):
            zero, one = in_ref[c, y].astype(F32), in_ref[c, ny + y].astype(F32)
            a = jnp.where(swap, one, zero)
            b = jnp.where(swap, zero, one)
            top = jnp.where(first, a, pltpu.roll(b, half, 1))
            bottom = jnp.where(first, pltpu.roll(a, half, 1), b)
            out_ref[c, :deep, y * 2 * half : (y + 1) * 2 * half] = top.astype(BF16)
            out_ref[c, deep:, y * 2 * half : (y + 1) * 2 * half] = bottom.astype(BF16)


def xor_pairs(size, k):
    return [(i, i ^ k) for i in range(size)]


def per_device(t_matrix, v_jacobi, channel_dims, owner_map):
    t, v = t_matrix[0], v_jacobi[0]
    rows, width = t.shape
    half = rows // 2
    groups, nzg, ny = lax.axis_size("chan"), lax.axis_size("zg"), lax.axis_size("y")
    zg, zp, y = lax.axis_index("zg"), lax.axis_index("zp"), lax.axis_index("y")

    near = lax.ppermute(t, "zp", xor_pairs(2, 1))
    side = [lax.ppermute(t, "y", xor_pairs(ny, k)) for k in range(1, ny)]
    shares = [t[:half], None]
    for k in range(1, nzg):
        shares.append(lax.ppermute(t[:half], "zg", xor_pairs(nzg, k)))
        shares.append(lax.ppermute(t[half:], ("zg", "zp"), xor_pairs(2 * nzg, 2 * k + 1)))
    shares[1] = near[half:]
    cross = [lax.ppermute(near, "y", xor_pairs(ny, k)) for k in range(1, ny)]

    owners = jnp.arange(groups, dtype=jnp.int32)
    source = jnp.sum(owners[None, :] * (owner_map[None, :] == owners[:, None]).astype(jnp.int32), axis=1)
    share_at = source ^ (zg * 2 + zp)
    ry = np.arange(ny)
    row_at = [zp * ny + (y ^ ry), (1 - zp) * ny + (y ^ ry)]
    order = jnp.concatenate([row_at[0], row_at[1]]).astype(jnp.int32)
    place = jnp.concatenate([share_at.astype(jnp.int32), order])
    swap = jnp.sum(jnp.where(owners == lax.axis_index("chan"), source, 0)) & 1

    lefts = [t] + side + [near]
    smem, vmem = pl.BlockSpec(memory_space=pltpu.SMEM), pl.BlockSpec(memory_space=pltpu.VMEM)
    made = pl.pallas_call(
        weights_kernel,
        out_shape=[jax.ShapeDtypeStruct((width, width), BF16)]
        + [jax.ShapeDtypeStruct((rows, width), BF16)] * len(lefts),
        in_specs=[smem] + [vmem] * (1 + len(lefts)),
        out_specs=[vmem] * (1 + len(lefts)),
        compiler_params=pltpu.CompilerParams(vmem_limit_bytes=VMEM_LIMIT),
        cost_estimate=pl.CostEstimate(
            flops=2 * rows * width * width * len(lefts) + 4 * width * width,
            bytes_accessed=4 * width * width + 4 * rows * width * len(lefts),
            transcendentals=0,
        ),
    )(channel_dims, v, *lefts)
    vm, w = made[0], made[1:]
    n_t = len(cross)
    tiles = pl.pallas_call(
        functools.partial(tiles_kernel, len(w), n_t, len(shares), half),
        out_shape=jax.ShapeDtypeStruct((groups, 2 * ny, rows // 2, 2 * half), BF16),
        in_specs=[smem] + [vmem] * (len(w) + n_t + 1 + len(shares)),
        out_specs=vmem,
        scratch_shapes=[
            pltpu.VMEM((len(shares), half, width), BF16),
            pltpu.VMEM((groups * half, width), BF16),
        ],
        compiler_params=pltpu.CompilerParams(vmem_limit_bytes=VMEM_LIMIT),
        cost_estimate=pl.CostEstimate(
            flops=2 * rows * width * (width * n_t + groups * half * 2 * ny),
            bytes_accessed=2 * width * width + 4 * rows * width * 2 * ny,
            transcendentals=0,
        ),
    )(place, *w, *cross, vm, *shares)
    sent = tiles.reshape(groups * 2 * ny, rows // 2, 2 * half)
    got = lax.all_to_all(sent, ("chan", "zp", "y"), split_axis=0, concat_axis=0, tiled=True)
    got = got.reshape(groups, 2 * ny, rows // 2, 2 * half)
    out = pl.pallas_call(
        functools.partial(place_kernel, ny, half),
        out_shape=jax.ShapeDtypeStruct((groups, rows, ny * rows), BF16),
        in_specs=[smem, vmem],
        out_specs=vmem,
        compiler_params=pltpu.CompilerParams(vmem_limit_bytes=VMEM_LIMIT),
    )(swap.reshape(1), got)
    return out[None]


def solution(mesh):
    chan, blk = mesh.shape["chan"], mesh.shape["blk"]

    def whole(t_matrix, v_jacobi, channel_dims, owner_map):
        block_cols = t_matrix.shape[1] // chan
        ny = block_cols * blk // t_matrix.shape[1]
        inner = Mesh(mesh.devices.reshape(chan, blk // (2 * ny), 2, ny), ("chan", "zg", "zp", "y"))
        line = ("zg", "zp", "y")
        return jax.shard_map(
            per_device,
            mesh=inner,
            in_specs=(P("chan", line, None), P("chan", None, None), P("chan"), P()),
            out_specs=P("chan", None, line, None),
            check_vma=False,
        )(t_matrix, v_jacobi, channel_dims, owner_map)

    return whole
```

```python
import functools

import jax
import jax.numpy as jnp
from jax import lax
from jax.experimental import pallas as pl
from jax.experimental.pallas import tpu as pltpu
from jax.sharding import Mesh, PartitionSpec as P

F32 = jnp.float32
BF16 = jnp.bfloat16
VMEM_LIMIT = 48 * 1024 * 1024
WEIGHT = 10**11


def dot_nt(a, b):
    return lax.dot_general(a, b, (((1,), (1,)), ((), ())), preferred_element_type=F32)


def first_kernel(live_ref, v_ref, *refs):
    n_rows = (len(refs) - 1) // 2
    t_refs, vm_ref, w_refs = refs[:n_rows], refs[n_rows], refs[n_rows + 1 :]
    width = v_ref.shape[0]
    tile = min(256, width)
    live = live_ref[0]
    for i in range(0, width, tile):
        row_live = lax.broadcasted_iota(jnp.int32, (tile, tile), 0) + i < live
        for j in range(0, width, tile):
            col_live = lax.broadcasted_iota(jnp.int32, (tile, tile), 1) + j < live
            here = v_ref[i : i + tile, j : j + tile].astype(F32)
            there = v_ref[j : j + tile, i : i + tile].astype(F32)
            mean = (here + there.T) * 0.5
            vm_ref[i : i + tile, j : j + tile] = jnp.where(row_live & col_live, mean, 0.0).astype(BF16)
    for t_ref, w_ref in zip(t_refs, w_refs):
        w_ref[...] = jnp.dot(t_ref[...], vm_ref[...], preferred_element_type=F32).astype(BF16)


def tiles_kernel(n_w, n_t, half, owner_ref, *refs):
    w_refs, t_refs, vm_ref = refs[:n_w], refs[n_w : n_w + n_t], refs[n_w + n_t]
    near_ref, h_refs, (out_ref, left, picked) = refs[n_w + n_t + 1], refs[n_w + n_t + 2 : -3], refs[-3:]
    groups = len(h_refs) + 1
    rows = w_refs[0].shape[0]
    plane, line = lax.axis_index("zg") * 2 + lax.axis_index("zp"), lax.axis_index("y")
    ny = lax.axis_size("y")
    of_near = near_ref.at[pl.ds(pl.multiple_of((plane % 2) * half, half), half), :]
    for k, h_ref in enumerate([h_refs[0], of_near, *h_refs[1:]]):
        d = owner_ref[plane ^ k]
        picked[pl.ds(pl.multiple_of(d * half, half), half), :] = h_ref[...]
    for k, w_ref in enumerate(w_refs):
        left[k * rows : (k + 1) * rows, :] = w_ref[...]
    for k, t_ref in enumerate(t_refs):
        w = jnp.dot(t_ref[...], vm_ref[...], preferred_element_type=F32)
        left[(n_w + k) * rows : (n_w + k + 1) * rows, :] = w.astype(BF16)
    first = lax.broadcasted_iota(jnp.int32, (rows // 2, 2 * half), 1) < half
    step = min(4 * half, groups * half)
    for at in range(0, groups * half, step):
        both = dot_nt(left[...], picked[at : at + step, :])
        for k in range(n_w + n_t):
            place = ((plane % 2) ^ (k // ny)) * ny + (line ^ (k % ny))
            for pair in range(step // (2 * half)):
                part = both[k * rows : (k + 1) * rows, pair * 2 * half : (pair + 1) * 2 * half]
                top, bottom = part[: rows // 2], part[rows // 2 :]
                even = jnp.where(first, top, pltpu.roll(bottom, half, 1))
                odd = jnp.where(first, pltpu.roll(top, half, 1), bottom)
                slot = at // half + 2 * pair
                out_ref[slot, place] = even.astype(BF16)
                out_ref[slot + 1, place] = odd.astype(BF16)


def place_kernel(ny, half, in_ref, out_ref, placed, sems):
    channels = in_ref.shape[0]
    deep = in_ref.shape[2]
    first = lax.broadcasted_iota(jnp.int32, (deep, 2 * half), 1) < half
    copies = []
    for c in range(channels):
        for y in range(ny):
            a, b = in_ref[c, y].astype(F32), in_ref[c, ny + y].astype(F32)
            top = jnp.where(first, a, pltpu.roll(b, half, 1))
            bottom = jnp.where(first, pltpu.roll(a, half, 1), b)
            placed[c, :deep, y * 2 * half : (y + 1) * 2 * half] = top.astype(BF16)
            placed[c, deep:, y * 2 * half : (y + 1) * 2 * half] = bottom.astype(BF16)
        copies.append(pltpu.make_async_copy(placed.at[c], out_ref.at[c], sems.at[c]))
        copies[-1].start()
    for copy in copies:
        copy.wait()


def xor_pairs(size, k):
    return [(i, i ^ k) for i in range(size)]


def call(kernel, out_shape, operands, scratch=(), scalars=0, out_space=pltpu.VMEM):
    outs = out_shape if isinstance(out_shape, list) else [out_shape]
    out_spec = pl.BlockSpec(memory_space=out_space)
    return pl.pallas_call(
        kernel,
        out_shape=out_shape,
        in_specs=[pl.BlockSpec(memory_space=pltpu.SMEM)] * scalars
        + [pl.BlockSpec(memory_space=pltpu.VMEM)] * (len(operands) - scalars),
        out_specs=[out_spec] * len(outs) if isinstance(out_shape, list) else out_spec,
        scratch_shapes=list(scratch),
        compiler_params=pltpu.CompilerParams(vmem_limit_bytes=VMEM_LIMIT),
        cost_estimate=pl.CostEstimate(flops=WEIGHT, bytes_accessed=WEIGHT, transcendentals=0),
    )(*operands)


def per_device(t_matrix, v_jacobi, channel_dims, owner_map):
    t, v = t_matrix[0], v_jacobi[0]
    rows, width = t.shape
    half = rows // 2
    groups, nzg, ny = lax.axis_size("chan"), lax.axis_size("zg"), lax.axis_size("y")
    block = jax.ShapeDtypeStruct((rows, width), BF16)

    parity = lax.axis_index("zp")
    near = lax.ppermute(t, "zp", xor_pairs(2, 1))
    side = [lax.ppermute(t, "y", xor_pairs(ny, k)) for k in range(1, ny)]
    same = lax.dynamic_slice_in_dim(t, parity * half, half)
    other = lax.dynamic_slice_in_dim(t, (1 - parity) * half, half)
    shares = [same]
    for k in range(1, nzg):
        shares.append(lax.ppermute(same, "zg", xor_pairs(nzg, k)))
        shares.append(lax.ppermute(other, ("zg", "zp"), xor_pairs(2 * nzg, 2 * k + 1)))
    cross = [lax.ppermute(near, "y", xor_pairs(ny, k)) for k in range(1, ny)]

    early = side + [near]
    made = call(
        first_kernel,
        [jax.ShapeDtypeStruct((width, width), BF16)] + [block] * (1 + len(early)),
        [channel_dims, v, t] + early,
        scalars=1,
    )
    vm, lefts = made[0], list(made[1:])
    tiles = call(
        functools.partial(tiles_kernel, len(lefts), len(cross), half),
        jax.ShapeDtypeStruct((groups, 2 * ny, rows // 2, 2 * half), BF16),
        [owner_map] + lefts + cross + [vm, near] + shares,
        scratch=[pltpu.VMEM((2 * ny * rows, width), BF16), pltpu.VMEM((groups * half, width), BF16)],
        scalars=1,
    )
    sent = tiles.reshape(groups * 2 * ny, rows // 2, 2 * half)
    got = lax.all_to_all(sent, ("chan", "zp", "y"), split_axis=0, concat_axis=0, tiled=True)
    got = got.reshape(groups, 2 * ny, rows // 2, 2 * half)
    out = call(
        functools.partial(place_kernel, ny, half),
        jax.ShapeDtypeStruct((groups, rows, ny * rows), BF16),
        [got],
        scratch=[pltpu.VMEM((groups, rows, ny * rows), BF16), pltpu.SemaphoreType.DMA((groups,))],
        out_space=pl.ANY,
    )
    return out[None]


def solution(mesh):
    chan, blk = mesh.shape["chan"], mesh.shape["blk"]

    def whole(t_matrix, v_jacobi, channel_dims, owner_map):
        block_cols = t_matrix.shape[1] // chan
        ny = block_cols * blk // t_matrix.shape[1]
        inner = Mesh(mesh.devices.reshape(chan, blk // (2 * ny), 2, ny), ("chan", "zg", "zp", "y"))
        line = ("zg", "zp", "y")
        return jax.shard_map(
            per_device,
            mesh=inner,
            in_specs=(P("chan", line, None), P("chan", None, None), P("chan"), P()),
            out_specs=P("chan", None, line, None),
            check_vma=False,
        )(t_matrix, v_jacobi, channel_dims, owner_map)

    return whole
```

```python
import functools

import jax
import jax.numpy as jnp
from jax import lax
from jax.experimental import pallas as pl
from jax.experimental.pallas import tpu as pltpu
from jax.sharding import Mesh, PartitionSpec as P

F32 = jnp.float32
BF16 = jnp.bfloat16
VMEM_LIMIT = 48 * 1024 * 1024
WEIGHT = 10**11


def dot_nt(a, b):
    return lax.dot_general(a, b, (((1,), (1,)), ((), ())), preferred_element_type=F32)


def first_kernel(live_ref, v_ref, *refs):
    t_refs, (vm_ref, w_ref) = refs[:-2], refs[-2:]
    width = v_ref.shape[0]
    tile = min(256, width)
    live = live_ref[0]
    for i in range(0, width, tile):
        row_live = lax.broadcasted_iota(jnp.int32, (tile, tile), 0) + i < live
        for j in range(0, width, tile):
            col_live = lax.broadcasted_iota(jnp.int32, (tile, tile), 1) + j < live
            here = v_ref[i : i + tile, j : j + tile].astype(F32)
            there = v_ref[j : j + tile, i : i + tile].astype(F32)
            mean = (here + there.T) * 0.5
            vm_ref[i : i + tile, j : j + tile] = jnp.where(row_live & col_live, mean, 0.0).astype(BF16)
    rows = t_refs[0].shape[0]
    for k, t_ref in enumerate(t_refs):
        w = jnp.dot(t_ref[...], vm_ref[...], preferred_element_type=F32)
        w_ref[k * rows : (k + 1) * rows, :] = w.astype(BF16)


def tiles_kernel(half, owner_ref, w_ref, vm_ref, near_ref, *refs):
    zg, zp, line = lax.axis_index("zg"), lax.axis_index("zp"), lax.axis_index("y")
    plane, ny = zg * 2 + zp, lax.axis_size("y")
    groups = 2 * lax.axis_size("zg")
    cross_refs, h_refs, (out_ref, picked) = refs[: ny - 1], refs[ny - 1 : -2], refs[-2:]
    rows = near_ref.shape[0]
    of_near = near_ref.at[pl.ds(pl.multiple_of(zp * half, half), half), :]
    for k, h_ref in enumerate([h_refs[0], of_near, *h_refs[1:]]):
        d = jnp.sum(jnp.where(lax.broadcasted_iota(jnp.int32, owner_ref.shape, 1) == (plane ^ k), owner_ref[...], 0))
        picked[pl.ds(pl.multiple_of(d * half, half), half), :] = h_ref[...]
    first = lax.broadcasted_iota(jnp.int32, (rows // 2, 2 * half), 1) < half
    step = min(4 * half, groups * half)

    def tiles(left, k_first):
        for at in range(0, groups * half, step):
            both = dot_nt(left, picked[at : at + step, :])
            for i in range(left.shape[0] // rows):
                k = k_first + i
                place = (zp ^ (k // ny)) * ny + (line ^ (k % ny))
                for pair in range(step // (2 * half)):
                    part = both[i * rows : (i + 1) * rows, pair * 2 * half : (pair + 1) * 2 * half]
                    top, bottom = part[: rows // 2], part[rows // 2 :]
                    even = jnp.where(first, top, pltpu.roll(bottom, half, 1))
                    odd = jnp.where(first, pltpu.roll(top, half, 1), bottom)
                    slot = at // half + 2 * pair
                    out_ref[slot, place] = even.astype(BF16)
                    out_ref[slot + 1, place] = odd.astype(BF16)

    ws = []
    for k, t_ref in enumerate(cross_refs):
        w = jnp.dot(t_ref[...], vm_ref[...], preferred_element_type=F32).astype(BF16)
        ws.append(w)
    tiles(jnp.concatenate([w_ref[...]] + ws, axis=0), 0)


def place_kernel(ny, half, in_ref, out_ref, placed, sems):
    channels = in_ref.shape[0]
    deep = in_ref.shape[2]
    first = lax.broadcasted_iota(jnp.int32, (deep, 2 * half), 1) < half
    copies = []
    for c in range(channels):
        for y in range(ny):
            a, b = in_ref[c, y].astype(F32), in_ref[c, ny + y].astype(F32)
            top = jnp.where(first, a, pltpu.roll(b, half, 1))
            bottom = jnp.where(first, pltpu.roll(a, half, 1), b)
            placed[c, :deep, y * 2 * half : (y + 1) * 2 * half] = top.astype(BF16)
            placed[c, deep:, y * 2 * half : (y + 1) * 2 * half] = bottom.astype(BF16)
        copies.append(pltpu.make_async_copy(placed.at[c], out_ref.at[c], sems.at[c]))
        copies[-1].start()
    for copy in copies:
        copy.wait()


def xor_pairs(size, k):
    return [(i, i ^ k) for i in range(size)]


def call(kernel, out_shape, operands, scratch=(), scalars=0, out_space=pltpu.VMEM):
    outs = out_shape if isinstance(out_shape, list) else [out_shape]
    out_spec = pl.BlockSpec(memory_space=out_space)
    return pl.pallas_call(
        kernel,
        out_shape=out_shape,
        in_specs=[pl.BlockSpec(memory_space=pltpu.SMEM)] * scalars
        + [pl.BlockSpec(memory_space=pltpu.VMEM)] * (len(operands) - scalars),
        out_specs=[out_spec] * len(outs) if isinstance(out_shape, list) else out_spec,
        scratch_shapes=list(scratch),
        compiler_params=pltpu.CompilerParams(vmem_limit_bytes=VMEM_LIMIT),
        cost_estimate=pl.CostEstimate(flops=WEIGHT, bytes_accessed=WEIGHT, transcendentals=0),
    )(*operands)


def lab_tiles(t, v, channel_dims, owner_map):
    rows, width = t.shape
    half = rows // 2
    groups, nzg, ny = lax.axis_size("chan"), lax.axis_size("zg"), lax.axis_size("y")
    parity = lax.axis_index("zp")
    near = lax.ppermute(t, "zp", xor_pairs(2, 1))
    side = [lax.ppermute(t, "y", xor_pairs(ny, k)) for k in range(1, ny)]
    same = lax.dynamic_slice_in_dim(t, parity * half, half)
    other = lax.dynamic_slice_in_dim(t, (1 - parity) * half, half)
    shares = [same]
    for k in range(1, nzg):
        shares.append(lax.ppermute(same, "zg", xor_pairs(nzg, k)))
        shares.append(lax.ppermute(other, ("zg", "zp"), xor_pairs(2 * nzg, 2 * k + 1)))
    cross = [lax.ppermute(near, "y", xor_pairs(ny, k)) for k in range(1, ny)]

    lefts = [t] + side + [near]
    vm, w = call(
        first_kernel,
        [jax.ShapeDtypeStruct((width, width), BF16), jax.ShapeDtypeStruct((len(lefts) * rows, width), BF16)],
        [channel_dims, v] + lefts,
        scalars=1,
    )
    return call(
        functools.partial(tiles_kernel, half),
        jax.ShapeDtypeStruct((groups, 2 * ny, rows // 2, 2 * half), BF16),
        [owner_map[None, :], w, vm, near] + cross + shares,
        scratch=[pltpu.VMEM((groups * half, width), BF16)],
    )


def per_device(t_matrix, v_jacobi, channel_dims, owner_map):
    t, v = t_matrix[0], v_jacobi[0]
    rows = t.shape[0]
    half = rows // 2
    groups, ny = lax.axis_size("chan"), lax.axis_size("y")
    tiles = lab_tiles(t, v, channel_dims, owner_map)

    sent = tiles.reshape(groups * 2 * ny, rows // 2, 2 * half)
    got = lax.all_to_all(sent, ("chan", "zp", "y"), split_axis=0, concat_axis=0, tiled=True)
    got = got.reshape(groups, 2 * ny, rows // 2, 2 * half)
    out = call(
        functools.partial(place_kernel, ny, half),
        jax.ShapeDtypeStruct((groups, rows, ny * rows), BF16),
        [got],
        scratch=[pltpu.VMEM((groups, rows, ny * rows), BF16), pltpu.SemaphoreType.DMA((groups,))],
        out_space=pl.ANY,
    )
    return out[None]


def solution(mesh):
    chan, blk = mesh.shape["chan"], mesh.shape["blk"]

    def whole(t_matrix, v_jacobi, channel_dims, owner_map):
        block_cols = t_matrix.shape[1] // chan
        ny = block_cols * blk // t_matrix.shape[1]
        inner = Mesh(mesh.devices.reshape(chan, blk // (2 * ny), 2, ny), ("chan", "zg", "zp", "y"))
        line = ("zg", "zp", "y")
        return jax.shard_map(
            per_device,
            mesh=inner,
            in_specs=(P("chan", line, None), P("chan", None, None), P("chan"), P()),
            out_specs=P("chan", None, line, None),
            check_vma=False,
        )(t_matrix, v_jacobi, channel_dims, owner_map)

    return whole
```

```python
import functools

import jax
import jax.numpy as jnp
from jax import lax
from jax.experimental import pallas as pl
from jax.experimental.pallas import tpu as pltpu
from jax.sharding import Mesh, PartitionSpec as P

F32 = jnp.float32
BF16 = jnp.bfloat16
VMEM_LIMIT = 48 * 1024 * 1024
WEIGHT = 10**11


def dot_nt(a, b):
    return lax.dot_general(a, b, (((1,), (1,)), ((), ())), preferred_element_type=F32)


def order_kernel(in_ref, out_ref):
    plane = lax.axis_index("zg") * 2 + lax.axis_index("zp")
    out_ref[...] = in_ref[...] ^ plane


def first_kernel(live_ref, v_ref, *refs):
    t_refs, (vm_ref, w_ref) = refs[:-2], refs[-2:]
    width = v_ref.shape[0]
    tile = min(256, width)
    live = live_ref[0]
    for i in range(0, width, tile):
        row_live = lax.broadcasted_iota(jnp.int32, (tile, tile), 0) + i < live
        for j in range(0, width, tile):
            col_live = lax.broadcasted_iota(jnp.int32, (tile, tile), 1) + j < live
            here = v_ref[i : i + tile, j : j + tile].astype(F32)
            there = v_ref[j : j + tile, i : i + tile].astype(F32)
            mean = (here + there.T) * 0.5
            vm_ref[i : i + tile, j : j + tile] = jnp.where(row_live & col_live, mean, 0.0).astype(BF16)
    rows = t_refs[0].shape[0]
    for k, t_ref in enumerate(t_refs):
        w = jnp.dot(t_ref[...], vm_ref[...], preferred_element_type=F32)
        w_ref[k * rows : (k + 1) * rows, :] = w.astype(BF16)


def tiles_kernel(half, order_ref, owner_ref, w_ref, vm_ref, near_ref, *refs):
    zg, zp, line = lax.axis_index("zg"), lax.axis_index("zp"), lax.axis_index("y")
    plane, ny = zg * 2 + zp, lax.axis_size("y")
    groups = 2 * lax.axis_size("zg")
    cross_refs, h_refs, (out_ref, picked) = refs[: ny - 1], refs[ny - 1 : -2], refs[-2:]
    rows = near_ref.shape[0]
    of_near = near_ref.at[pl.ds(pl.multiple_of(zp * half, half), half), :]
    for k, h_ref in enumerate([h_refs[0], of_near, *h_refs[1:]]):
        d = jnp.sum(jnp.where(order_ref[...] == k, owner_ref[...], 0))
        picked[pl.ds(pl.multiple_of(d * half, half), half), :] = h_ref[...]
    first = lax.broadcasted_iota(jnp.int32, (rows // 2, 2 * half), 1) < half
    step = min(4 * half, groups * half)

    def tiles(left, k_first):
        for at in range(0, groups * half, step):
            both = dot_nt(left, picked[at : at + step, :])
            for i in range(left.shape[0] // rows):
                k = k_first + i
                place = (zp ^ (k // ny)) * ny + (line ^ (k % ny))
                for pair in range(step // (2 * half)):
                    part = both[i * rows : (i + 1) * rows, pair * 2 * half : (pair + 1) * 2 * half]
                    top, bottom = part[: rows // 2], part[rows // 2 :]
                    even = jnp.where(first, top, pltpu.roll(bottom, half, 1))
                    odd = jnp.where(first, pltpu.roll(top, half, 1), bottom)
                    slot = at // half + 2 * pair
                    out_ref[slot, place] = even.astype(BF16)
                    out_ref[slot + 1, place] = odd.astype(BF16)

    ws = []
    for k, t_ref in enumerate(cross_refs):
        w = jnp.dot(t_ref[...], vm_ref[...], preferred_element_type=F32).astype(BF16)
        ws.append(w)
    tiles(jnp.concatenate([w_ref[...]] + ws, axis=0), 0)


def place_kernel(ny, half, in_ref, out_ref, placed, sems):
    channels = in_ref.shape[0]
    deep = in_ref.shape[2]
    first = lax.broadcasted_iota(jnp.int32, (deep, 2 * half), 1) < half
    copies = []
    for c in range(channels):
        for y in range(ny):
            a, b = in_ref[c, y].astype(F32), in_ref[c, ny + y].astype(F32)
            top = jnp.where(first, a, pltpu.roll(b, half, 1))
            bottom = jnp.where(first, pltpu.roll(a, half, 1), b)
            placed[c, :deep, y * 2 * half : (y + 1) * 2 * half] = top.astype(BF16)
            placed[c, deep:, y * 2 * half : (y + 1) * 2 * half] = bottom.astype(BF16)
        copies.append(pltpu.make_async_copy(placed.at[c], out_ref.at[c], sems.at[c]))
        copies[-1].start()
    for copy in copies:
        copy.wait()


def xor_pairs(size, k):
    return [(i, i ^ k) for i in range(size)]


def turn_pairs(channels, ny, k):
    pairs = []
    for c in range(channels):
        for p in range(2):
            for y in range(ny):
                to = (1 - p) * ny + y if c % 2 else p * ny + (y ^ k)
                pairs.append(((2 * c + p) * ny + y, 2 * c * ny + to))
    return pairs


def call(kernel, out_shape, operands, scratch=(), scalars=0, out_space=pltpu.VMEM, weight=WEIGHT):
    outs = out_shape if isinstance(out_shape, list) else [out_shape]
    out_spec = pl.BlockSpec(memory_space=out_space)
    return pl.pallas_call(
        kernel,
        out_shape=out_shape,
        in_specs=[pl.BlockSpec(memory_space=pltpu.SMEM)] * scalars
        + [pl.BlockSpec(memory_space=pltpu.VMEM)] * (len(operands) - scalars),
        out_specs=[out_spec] * len(outs) if isinstance(out_shape, list) else out_spec,
        scratch_shapes=list(scratch),
        compiler_params=pltpu.CompilerParams(vmem_limit_bytes=VMEM_LIMIT),
        cost_estimate=pl.CostEstimate(flops=weight, bytes_accessed=weight, transcendentals=0),
    )(*operands)


def lab_tiles(t, v, channel_dims, owner_map):
    rows, width = t.shape
    half = rows // 2
    groups, nzg, ny = lax.axis_size("chan"), lax.axis_size("zg"), lax.axis_size("y")
    parity = lax.axis_index("zp")
    near = lax.ppermute(t, "zp", xor_pairs(2, 1))
    side = [lax.ppermute(t, "y", xor_pairs(ny, k)) for k in range(1, ny)]
    same = lax.dynamic_slice_in_dim(t, parity * half, half)
    other = lax.dynamic_slice_in_dim(t, (1 - parity) * half, half)
    shares = [same]
    for k in range(1, nzg):
        shares.append(lax.ppermute(same, "zg", xor_pairs(nzg, k)))
        shares.append(lax.ppermute(other, ("zg", "zp"), xor_pairs(2 * nzg, 2 * k + 1)))
    odd = lax.axis_index("chan") % 2 > 0
    planes, near = lax.optimization_barrier((jnp.arange(groups, dtype=jnp.int32)[None, :], near))
    order = call(order_kernel, jax.ShapeDtypeStruct((1, groups), jnp.int32), [planes], weight=1)
    near, order = lax.optimization_barrier((near, order))
    cross = [
        lax.ppermute(jnp.where(odd, other_line, near), ("chan", "zp", "y"), turn_pairs(groups, ny, k))
        for k, other_line in enumerate(side, 1)
    ]

    lefts = [t] + side + [near]
    vm, w = call(
        first_kernel,
        [jax.ShapeDtypeStruct((width, width), BF16), jax.ShapeDtypeStruct((len(lefts) * rows, width), BF16)],
        [channel_dims, v] + lefts,
        scalars=1,
    )
    return call(
        functools.partial(tiles_kernel, half),
        jax.ShapeDtypeStruct((groups, 2 * ny, rows // 2, 2 * half), BF16),
        [order, owner_map[None, :], w, vm, near] + cross + shares,
        scratch=[pltpu.VMEM((groups * half, width), BF16)],
    )


def per_device(t_matrix, v_jacobi, channel_dims, owner_map):
    t, v = t_matrix[0], v_jacobi[0]
    rows = t.shape[0]
    half = rows // 2
    groups, ny = lax.axis_size("chan"), lax.axis_size("y")
    tiles = lab_tiles(t, v, channel_dims, owner_map)

    sent = tiles.reshape(groups * 2 * ny, rows // 2, 2 * half)
    got = lax.all_to_all(sent, ("chan", "zp", "y"), split_axis=0, concat_axis=0, tiled=True)
    got = got.reshape(groups, 2 * ny, rows // 2, 2 * half)
    out = call(
        functools.partial(place_kernel, ny, half),
        jax.ShapeDtypeStruct((groups, rows, ny * rows), BF16),
        [got],
        scratch=[pltpu.VMEM((groups, rows, ny * rows), BF16), pltpu.SemaphoreType.DMA((groups,))],
        out_space=pl.ANY,
    )
    return out[None]


def solution(mesh):
    chan, blk = mesh.shape["chan"], mesh.shape["blk"]

    def whole(t_matrix, v_jacobi, channel_dims, owner_map):
        block_cols = t_matrix.shape[1] // chan
        ny = block_cols * blk // t_matrix.shape[1]
        inner = Mesh(mesh.devices.reshape(chan, blk // (2 * ny), 2, ny), ("chan", "zg", "zp", "y"))
        line = ("zg", "zp", "y")
        return jax.shard_map(
            per_device,
            mesh=inner,
            in_specs=(P("chan", line, None), P("chan", None, None), P("chan"), P()),
            out_specs=P("chan", None, line, None),
            check_vma=False,
        )(t_matrix, v_jacobi, channel_dims, owner_map)

    return whole
```

```python
import functools

import jax
import jax.numpy as jnp
from jax import lax
from jax.experimental import pallas as pl
from jax.experimental.pallas import tpu as pltpu
from jax.sharding import Mesh, PartitionSpec as P

F32 = jnp.float32
BF16 = jnp.bfloat16
VMEM_LIMIT = 48 * 1024 * 1024
WEIGHT = 10**11


def dot_nt(a, b):
    return lax.dot_general(a, b, (((1,), (1,)), ((), ())), preferred_element_type=F32)


def order_kernel(in_ref, out_ref):
    plane = lax.axis_index("zg") * 2 + lax.axis_index("zp")
    out_ref[...] = in_ref[...] ^ plane


def first_kernel(live_ref, v_ref, *refs):
    t_refs, (vm_ref, w_ref) = refs[:-2], refs[-2:]
    width = v_ref.shape[0]
    tile = min(256, width)
    live = live_ref[0]
    for i in range(0, width, tile):
        row_live = lax.broadcasted_iota(jnp.int32, (tile, tile), 0) + i < live
        for j in range(0, width, tile):
            col_live = lax.broadcasted_iota(jnp.int32, (tile, tile), 1) + j < live
            here = v_ref[i : i + tile, j : j + tile].astype(F32)
            there = v_ref[j : j + tile, i : i + tile].astype(F32)
            mean = (here + there.T) * 0.5
            vm_ref[i : i + tile, j : j + tile] = jnp.where(row_live & col_live, mean, 0.0).astype(BF16)
    rows = t_refs[0].shape[0]
    for k, t_ref in enumerate(t_refs):
        w = jnp.dot(t_ref[...], vm_ref[...], preferred_element_type=F32)
        w_ref[k * rows : (k + 1) * rows, :] = w.astype(BF16)


def tiles_kernel(half, order_ref, owner_ref, w_ref, vm_ref, near_ref, *refs):
    zg, zp, line = lax.axis_index("zg"), lax.axis_index("zp"), lax.axis_index("y")
    plane, ny = zg * 2 + zp, lax.axis_size("y")
    groups = 2 * lax.axis_size("zg")
    cross_refs, h_refs, (out_ref, picked) = refs[: ny - 1], refs[ny - 1 : -2], refs[-2:]
    rows = near_ref.shape[0]
    of_near = near_ref.at[pl.ds(pl.multiple_of(zp * half, half), half), :]
    for k, h_ref in enumerate([h_refs[0], of_near, *h_refs[1:]]):
        d = jnp.sum(jnp.where(order_ref[...] == k, owner_ref[...], 0))
        picked[pl.ds(pl.multiple_of(d * half, half), half), :] = h_ref[...]
    first = lax.broadcasted_iota(jnp.int32, (rows // 2, 2 * half), 1) < half
    step = min(4 * half, groups * half)

    def tiles(left, k_first):
        for at in range(0, groups * half, step):
            both = dot_nt(left, picked[at : at + step, :])
            for i in range(left.shape[0] // rows):
                k = k_first + i
                place = (zp ^ (k // ny)) * ny + (line ^ (k % ny))
                for pair in range(step // (2 * half)):
                    part = both[i * rows : (i + 1) * rows, pair * 2 * half : (pair + 1) * 2 * half]
                    top, bottom = part[: rows // 2], part[rows // 2 :]
                    even = jnp.where(first, top, pltpu.roll(bottom, half, 1))
                    odd = jnp.where(first, pltpu.roll(top, half, 1), bottom)
                    slot = at // half + 2 * pair
                    out_ref[slot, place] = even.astype(BF16)
                    out_ref[slot + 1, place] = odd.astype(BF16)

    ws = []
    for k, t_ref in enumerate(cross_refs):
        w = jnp.dot(t_ref[...], vm_ref[...], preferred_element_type=F32).astype(BF16)
        ws.append(w)
    tiles(jnp.concatenate([w_ref[...]] + ws, axis=0), 0)


def place_kernel(ny, half, in_ref, out_ref, placed, sems):
    channels = in_ref.shape[0]
    deep = in_ref.shape[2]
    first = lax.broadcasted_iota(jnp.int32, (deep, 2 * half), 1) < half
    copies = []
    for c in range(channels):
        for y in range(ny):
            a, b = in_ref[c, y].astype(F32), in_ref[c, ny + y].astype(F32)
            top = jnp.where(first, a, pltpu.roll(b, half, 1))
            bottom = jnp.where(first, pltpu.roll(a, half, 1), b)
            placed[c, :deep, y * 2 * half : (y + 1) * 2 * half] = top.astype(BF16)
            placed[c, deep:, y * 2 * half : (y + 1) * 2 * half] = bottom.astype(BF16)
        copies.append(pltpu.make_async_copy(placed.at[c], out_ref.at[c], sems.at[c]))
        copies[-1].start()
    for copy in copies:
        copy.wait()


def xor_pairs(size, k):
    return [(i, i ^ k) for i in range(size)]


def turn_pairs(channels, ny, k):
    pairs = []
    for c in range(channels):
        for p in range(2):
            for y in range(ny):
                to = (1 - p) * ny + y if c % 2 else p * ny + (y ^ k)
                pairs.append(((2 * c + p) * ny + y, 2 * c * ny + to))
    return pairs


def call(kernel, out_shape, operands, scratch=(), scalars=0, out_space=pltpu.VMEM, weight=WEIGHT):
    outs = out_shape if isinstance(out_shape, list) else [out_shape]
    out_spec = pl.BlockSpec(memory_space=out_space)
    return pl.pallas_call(
        kernel,
        out_shape=out_shape,
        in_specs=[pl.BlockSpec(memory_space=pltpu.SMEM)] * scalars
        + [pl.BlockSpec(memory_space=pltpu.VMEM)] * (len(operands) - scalars),
        out_specs=[out_spec] * len(outs) if isinstance(out_shape, list) else out_spec,
        scratch_shapes=list(scratch),
        compiler_params=pltpu.CompilerParams(vmem_limit_bytes=VMEM_LIMIT),
        cost_estimate=pl.CostEstimate(flops=weight, bytes_accessed=weight, transcendentals=0),
    )(*operands)


def lab_tiles(t, v, channel_dims, owner_map):
    rows, width = t.shape
    half = rows // 2
    groups, nzg, ny = lax.axis_size("chan"), lax.axis_size("zg"), lax.axis_size("y")
    parity = lax.axis_index("zp")
    near = lax.ppermute(t, "zp", xor_pairs(2, 1))
    side = [lax.ppermute(t, "y", xor_pairs(ny, k)) for k in range(1, ny)]
    same = lax.dynamic_slice_in_dim(t, parity * half, half)
    other = lax.dynamic_slice_in_dim(t, (1 - parity) * half, half)
    shares = [same]
    for k in range(1, nzg):
        shares.append(lax.ppermute(same, "zg", xor_pairs(nzg, k)))
        shares.append(lax.ppermute(other, ("zg", "zp"), xor_pairs(2 * nzg, 2 * k + 1)))
    odd = lax.axis_index("chan") % 2 > 0
    planes, near = lax.optimization_barrier((jnp.arange(groups, dtype=jnp.int32)[None, :], near))
    order = call(order_kernel, jax.ShapeDtypeStruct((1, groups), jnp.int32), [planes], weight=10**9)
    near, order = lax.optimization_barrier((near, order))
    cross = [
        lax.ppermute(jnp.where(odd, other_line, near), ("chan", "zp", "y"), turn_pairs(groups, ny, k))
        for k, other_line in enumerate(side, 1)
    ]

    lefts = [t] + side + [near]
    vm, w = call(
        first_kernel,
        [jax.ShapeDtypeStruct((width, width), BF16), jax.ShapeDtypeStruct((len(lefts) * rows, width), BF16)],
        [channel_dims, v] + lefts,
        scalars=1,
    )
    return call(
        functools.partial(tiles_kernel, half),
        jax.ShapeDtypeStruct((groups, 2 * ny, rows // 2, 2 * half), BF16),
        [order, owner_map[None, :], w, vm, near] + cross + shares,
        scratch=[pltpu.VMEM((groups * half, width), BF16)],
    )


def per_device(t_matrix, v_jacobi, channel_dims, owner_map):
    t, v = t_matrix[0], v_jacobi[0]
    rows = t.shape[0]
    half = rows // 2
    groups, ny = lax.axis_size("chan"), lax.axis_size("y")
    tiles = lab_tiles(t, v, channel_dims, owner_map)

    sent = tiles.reshape(groups * 2 * ny, rows // 2, 2 * half)
    got = lax.all_to_all(sent, ("chan", "zp", "y"), split_axis=0, concat_axis=0, tiled=True)
    got = got.reshape(groups, 2 * ny, rows // 2, 2 * half)
    out = call(
        functools.partial(place_kernel, ny, half),
        jax.ShapeDtypeStruct((groups, rows, ny * rows), BF16),
        [got],
        scratch=[pltpu.VMEM((groups, rows, ny * rows), BF16), pltpu.SemaphoreType.DMA((groups,))],
        out_space=pl.ANY,
    )
    return out[None]


def solution(mesh):
    chan, blk = mesh.shape["chan"], mesh.shape["blk"]

    def whole(t_matrix, v_jacobi, channel_dims, owner_map):
        block_cols = t_matrix.shape[1] // chan
        ny = block_cols * blk // t_matrix.shape[1]
        inner = Mesh(mesh.devices.reshape(chan, blk // (2 * ny), 2, ny), ("chan", "zg", "zp", "y"))
        line = ("zg", "zp", "y")
        return jax.shard_map(
            per_device,
            mesh=inner,
            in_specs=(P("chan", line, None), P("chan", None, None), P("chan"), P()),
            out_specs=P("chan", None, line, None),
            check_vma=False,
        )(t_matrix, v_jacobi, channel_dims, owner_map)

    return whole
```

```python
import functools

import jax
import jax.numpy as jnp
from jax import lax
from jax.experimental import pallas as pl
from jax.experimental.pallas import tpu as pltpu
from jax.sharding import Mesh, PartitionSpec as P

F32 = jnp.float32
BF16 = jnp.bfloat16
VMEM_LIMIT = 48 * 1024 * 1024
WEIGHT = 10**11


def dot_nt(a, b):
    return lax.dot_general(a, b, (((1,), (1,)), ((), ())), preferred_element_type=F32)


def order_kernel(in_ref, out_ref):
    plane = lax.axis_index("zg") * 2 + lax.axis_index("zp")
    out_ref[...] = in_ref[...] ^ plane


def first_kernel(live_ref, v_ref, *refs):
    t_refs, (vm_ref, w_ref) = refs[:-2], refs[-2:]
    width = v_ref.shape[0]
    tile = min(256, width)
    live = live_ref[0]
    for i in range(0, width, tile):
        row_live = lax.broadcasted_iota(jnp.int32, (tile, tile), 0) + i < live
        for j in range(0, width, tile):
            col_live = lax.broadcasted_iota(jnp.int32, (tile, tile), 1) + j < live
            here = v_ref[i : i + tile, j : j + tile].astype(F32)
            there = v_ref[j : j + tile, i : i + tile].astype(F32)
            mean = (here + there.T) * 0.5
            vm_ref[i : i + tile, j : j + tile] = jnp.where(row_live & col_live, mean, 0.0).astype(BF16)
    rows = t_refs[0].shape[0]
    for k, t_ref in enumerate(t_refs):
        w = jnp.dot(t_ref[...], vm_ref[...], preferred_element_type=F32)
        w_ref[k * rows : (k + 1) * rows, :] = w.astype(BF16)


def tiles_kernel(half, order_ref, owner_ref, w_ref, vm_ref, near_ref, *refs):
    zg, zp, line = lax.axis_index("zg"), lax.axis_index("zp"), lax.axis_index("y")
    plane, ny = zg * 2 + zp, lax.axis_size("y")
    groups = 2 * lax.axis_size("zg")
    cross_refs, h_refs, (out_ref, picked) = refs[: ny - 1], refs[ny - 1 : -2], refs[-2:]
    rows = near_ref.shape[0]
    of_near = near_ref.at[pl.ds(pl.multiple_of(zp * half, half), half), :]
    for k, h_ref in enumerate([h_refs[0], of_near, *h_refs[1:]]):
        d = jnp.sum(jnp.where(order_ref[...] == k, owner_ref[...], 0))
        picked[pl.ds(pl.multiple_of(d * half, half), half), :] = h_ref[...]
    first = lax.broadcasted_iota(jnp.int32, (rows // 2, 2 * half), 1) < half
    step = min(4 * half, groups * half)

    def tiles(left, k_first):
        for at in range(0, groups * half, step):
            both = dot_nt(left, picked[at : at + step, :])
            for i in range(left.shape[0] // rows):
                k = k_first + i
                place = (zp ^ (k // ny)) * ny + (line ^ (k % ny))
                for pair in range(step // (2 * half)):
                    part = both[i * rows : (i + 1) * rows, pair * 2 * half : (pair + 1) * 2 * half]
                    top, bottom = part[: rows // 2], part[rows // 2 :]
                    even = jnp.where(first, top, pltpu.roll(bottom, half, 1))
                    odd = jnp.where(first, pltpu.roll(top, half, 1), bottom)
                    slot = at // half + 2 * pair
                    out_ref[slot, place] = even.astype(BF16)
                    out_ref[slot + 1, place] = odd.astype(BF16)

    ws = []
    for k, t_ref in enumerate(cross_refs):
        w = jnp.dot(t_ref[...], vm_ref[...], preferred_element_type=F32).astype(BF16)
        ws.append(w)
    tiles(jnp.concatenate([w_ref[...]] + ws, axis=0), 0)


def place_kernel(ny, half, in_ref, out_ref, placed, sems):
    channels = in_ref.shape[0]
    deep = in_ref.shape[2]
    copies = []
    for c in range(channels):
        for y in range(ny):
            a, b = in_ref[c, y], in_ref[c, ny + y]
            at = slice(y * 2 * half, (y + 1) * 2 * half)
            placed[c, :deep, at] = jnp.concatenate([a[:, :half], b[:, :half]], axis=1)
            placed[c, deep:, at] = jnp.concatenate([a[:, half:], b[:, half:]], axis=1)
        copies.append(pltpu.make_async_copy(placed.at[c], out_ref.at[c], sems.at[c]))
        copies[-1].start()
    for copy in copies:
        copy.wait()


def xor_pairs(size, k):
    return [(i, i ^ k) for i in range(size)]


def turn_pairs(channels, ny, k):
    pairs = []
    for c in range(channels):
        for p in range(2):
            for y in range(ny):
                to = (1 - p) * ny + y if c % 2 else p * ny + (y ^ k)
                pairs.append(((2 * c + p) * ny + y, 2 * c * ny + to))
    return pairs


def call(kernel, out_shape, operands, scratch=(), scalars=0, out_space=pltpu.VMEM, weight=WEIGHT):
    outs = out_shape if isinstance(out_shape, list) else [out_shape]
    out_spec = pl.BlockSpec(memory_space=out_space)
    return pl.pallas_call(
        kernel,
        out_shape=out_shape,
        in_specs=[pl.BlockSpec(memory_space=pltpu.SMEM)] * scalars
        + [pl.BlockSpec(memory_space=pltpu.VMEM)] * (len(operands) - scalars),
        out_specs=[out_spec] * len(outs) if isinstance(out_shape, list) else out_spec,
        scratch_shapes=list(scratch),
        compiler_params=pltpu.CompilerParams(vmem_limit_bytes=VMEM_LIMIT),
        cost_estimate=pl.CostEstimate(flops=weight, bytes_accessed=weight, transcendentals=0),
    )(*operands)


def lab_tiles(t, v, channel_dims, owner_map):
    rows, width = t.shape
    half = rows // 2
    groups, nzg, ny = lax.axis_size("chan"), lax.axis_size("zg"), lax.axis_size("y")
    parity = lax.axis_index("zp")
    near = lax.ppermute(t, "zp", xor_pairs(2, 1))
    side = [lax.ppermute(t, "y", xor_pairs(ny, k)) for k in range(1, ny)]
    same = lax.dynamic_slice_in_dim(t, parity * half, half)
    other = lax.dynamic_slice_in_dim(t, (1 - parity) * half, half)
    shares = [same]
    for k in range(1, nzg):
        shares.append(lax.ppermute(same, "zg", xor_pairs(nzg, k)))
        shares.append(lax.ppermute(other, ("zg", "zp"), xor_pairs(2 * nzg, 2 * k + 1)))
    odd = lax.axis_index("chan") % 2 > 0
    planes, near = lax.optimization_barrier((jnp.arange(groups, dtype=jnp.int32)[None, :], near))
    order = call(order_kernel, jax.ShapeDtypeStruct((1, groups), jnp.int32), [planes], weight=10**9)
    near, order = lax.optimization_barrier((near, order))
    cross = [
        lax.ppermute(jnp.where(odd, other_line, near), ("chan", "zp", "y"), turn_pairs(groups, ny, k))
        for k, other_line in enumerate(side, 1)
    ]

    lefts = [t] + side + [near]
    vm, w = call(
        first_kernel,
        [jax.ShapeDtypeStruct((width, width), BF16), jax.ShapeDtypeStruct((len(lefts) * rows, width), BF16)],
        [channel_dims, v] + lefts,
        scalars=1,
    )
    return call(
        functools.partial(tiles_kernel, half),
        jax.ShapeDtypeStruct((groups, 2 * ny, rows // 2, 2 * half), BF16),
        [order, owner_map[None, :], w, vm, near] + cross + shares,
        scratch=[pltpu.VMEM((groups * half, width), BF16)],
    )


def per_device(t_matrix, v_jacobi, channel_dims, owner_map):
    t, v = t_matrix[0], v_jacobi[0]
    rows = t.shape[0]
    half = rows // 2
    groups, ny = lax.axis_size("chan"), lax.axis_size("y")
    tiles = lab_tiles(t, v, channel_dims, owner_map)

    sent = tiles.reshape(groups * 2 * ny, rows // 2, 2 * half)
    got = lax.all_to_all(sent, ("chan", "zp", "y"), split_axis=0, concat_axis=0, tiled=True)
    got = got.reshape(groups, 2 * ny, rows // 2, 2 * half)
    out = call(
        functools.partial(place_kernel, ny, half),
        jax.ShapeDtypeStruct((groups, rows, ny * rows), BF16),
        [got],
        scratch=[pltpu.VMEM((groups, rows, ny * rows), BF16), pltpu.SemaphoreType.DMA((groups,))],
        out_space=pl.ANY,
    )
    return out[None]


def solution(mesh):
    chan, blk = mesh.shape["chan"], mesh.shape["blk"]

    def whole(t_matrix, v_jacobi, channel_dims, owner_map):
        block_cols = t_matrix.shape[1] // chan
        ny = block_cols * blk // t_matrix.shape[1]
        inner = Mesh(mesh.devices.reshape(chan, blk // (2 * ny), 2, ny), ("chan", "zg", "zp", "y"))
        line = ("zg", "zp", "y")
        return jax.shard_map(
            per_device,
            mesh=inner,
            in_specs=(P("chan", line, None), P("chan", None, None), P("chan"), P()),
            out_specs=P("chan", None, line, None),
            check_vma=False,
        )(t_matrix, v_jacobi, channel_dims, owner_map)

    return whole
```

```python
import functools

import jax
import jax.numpy as jnp
from jax import lax
from jax.experimental import pallas as pl
from jax.experimental.pallas import tpu as pltpu
from jax.sharding import Mesh, PartitionSpec as P

F32 = jnp.float32
BF16 = jnp.bfloat16
VMEM_LIMIT = 48 * 1024 * 1024
WEIGHT = 10**11


def dot_nt(a, b):
    return lax.dot_general(a, b, (((1,), (1,)), ((), ())), preferred_element_type=F32)


def order_kernel(in_ref, out_ref):
    plane = lax.axis_index("zg") * 2 + lax.axis_index("zp")
    out_ref[...] = in_ref[...] ^ plane


def first_kernel(live_ref, v_ref, *refs):
    t_refs, (vm_ref, w_ref) = refs[:-2], refs[-2:]
    width = v_ref.shape[0]
    tile = min(256, width)
    live = live_ref[...]
    for i in range(0, width, tile):
        row_live = lax.broadcasted_iota(jnp.int32, (tile, tile), 0) + i < live
        for j in range(0, width, tile):
            col_live = lax.broadcasted_iota(jnp.int32, (tile, tile), 1) + j < live
            here = v_ref[i : i + tile, j : j + tile].astype(F32)
            there = v_ref[j : j + tile, i : i + tile].astype(F32)
            mean = (here + there.T) * 0.5
            vm_ref[i : i + tile, j : j + tile] = jnp.where(row_live & col_live, mean, 0.0).astype(BF16)
    rows = t_refs[0].shape[0]
    for k, t_ref in enumerate(t_refs):
        w = jnp.dot(t_ref[...], vm_ref[...], preferred_element_type=F32)
        w_ref[k * rows : (k + 1) * rows, :] = w.astype(BF16)


def tiles_kernel(half, order_ref, owner_ref, w_ref, vm_ref, near_ref, *refs):
    zg, zp, line = lax.axis_index("zg"), lax.axis_index("zp"), lax.axis_index("y")
    plane, ny = zg * 2 + zp, lax.axis_size("y")
    groups = 2 * lax.axis_size("zg")
    cross_refs, h_refs, (out_ref, picked) = refs[: ny - 1], refs[ny - 1 : -2], refs[-2:]
    rows = near_ref.shape[0]
    of_near = near_ref.at[pl.ds(pl.multiple_of(zp * half, half), half), :]
    for k, h_ref in enumerate([h_refs[0], of_near, *h_refs[1:]]):
        d = jnp.sum(jnp.where(order_ref[...] == k, owner_ref[...], 0))
        picked[pl.ds(pl.multiple_of(d * half, half), half), :] = h_ref[...]
    first = lax.broadcasted_iota(jnp.int32, (rows // 2, 2 * half), 1) < half
    step = min(4 * half, groups * half)

    def tiles(left, k_first):
        for at in range(0, groups * half, step):
            both = dot_nt(left, picked[at : at + step, :])
            for i in range(left.shape[0] // rows):
                k = k_first + i
                place = (zp ^ (k // ny)) * ny + (line ^ (k % ny))
                for pair in range(step // (2 * half)):
                    part = both[i * rows : (i + 1) * rows, pair * 2 * half : (pair + 1) * 2 * half]
                    top, bottom = part[: rows // 2], part[rows // 2 :]
                    even = jnp.where(first, top, pltpu.roll(bottom, half, 1))
                    odd = jnp.where(first, pltpu.roll(top, half, 1), bottom)
                    slot = at // half + 2 * pair
                    out_ref[slot, place] = even.astype(BF16)
                    out_ref[slot + 1, place] = odd.astype(BF16)

    ws = []
    for k, t_ref in enumerate(cross_refs):
        w = jnp.dot(t_ref[...], vm_ref[...], preferred_element_type=F32).astype(BF16)
        ws.append(w)
    tiles(jnp.concatenate([w_ref[...]] + ws, axis=0), 0)


def place_kernel(ny, half, in_ref, out_ref, placed, sems):
    channels = in_ref.shape[0]
    deep = in_ref.shape[2]
    copies = []
    for c in range(channels):
        for y in range(ny):
            a, b = in_ref[c, y], in_ref[c, ny + y]
            at = slice(y * 2 * half, (y + 1) * 2 * half)
            placed[c, :deep, at] = jnp.concatenate([a[:, :half], b[:, :half]], axis=1)
            placed[c, deep:, at] = jnp.concatenate([a[:, half:], b[:, half:]], axis=1)
        copies.append(pltpu.make_async_copy(placed.at[c], out_ref.at[c], sems.at[c]))
        copies[-1].start()
    for copy in copies:
        copy.wait()


def xor_pairs(size, k):
    return [(i, i ^ k) for i in range(size)]


def turn_pairs(channels, ny, k):
    pairs = []
    for c in range(channels):
        for p in range(2):
            for y in range(ny):
                to = (1 - p) * ny + y if c % 2 else p * ny + (y ^ k)
                pairs.append(((2 * c + p) * ny + y, 2 * c * ny + to))
    return pairs


def call(kernel, out_shape, operands, scratch=(), scalars=0, out_space=pltpu.VMEM, weight=WEIGHT):
    outs = out_shape if isinstance(out_shape, list) else [out_shape]
    out_spec = pl.BlockSpec(memory_space=out_space)
    return pl.pallas_call(
        kernel,
        out_shape=out_shape,
        in_specs=[pl.BlockSpec(memory_space=pltpu.SMEM)] * scalars
        + [pl.BlockSpec(memory_space=pltpu.VMEM)] * (len(operands) - scalars),
        out_specs=[out_spec] * len(outs) if isinstance(out_shape, list) else out_spec,
        scratch_shapes=list(scratch),
        compiler_params=pltpu.CompilerParams(vmem_limit_bytes=VMEM_LIMIT),
        cost_estimate=pl.CostEstimate(flops=weight, bytes_accessed=weight, transcendentals=0),
    )(*operands)


def lab_tiles(t, v, channel_dims, owner_map):
    rows, width = t.shape
    half = rows // 2
    groups, nzg, ny = lax.axis_size("chan"), lax.axis_size("zg"), lax.axis_size("y")
    parity = lax.axis_index("zp")
    near = lax.ppermute(t, "zp", xor_pairs(2, 1))
    side = [lax.ppermute(t, "y", xor_pairs(ny, k)) for k in range(1, ny)]
    same = lax.dynamic_slice_in_dim(t, parity * half, half)
    other = lax.dynamic_slice_in_dim(t, (1 - parity) * half, half)
    shares = [same]
    for k in range(1, nzg):
        shares.append(lax.ppermute(same, "zg", xor_pairs(nzg, k)))
        shares.append(lax.ppermute(other, ("zg", "zp"), xor_pairs(2 * nzg, 2 * k + 1)))
    odd = lax.axis_index("chan") % 2 > 0
    planes, near = lax.optimization_barrier((jnp.arange(groups, dtype=jnp.int32)[None, :], near))
    order = call(order_kernel, jax.ShapeDtypeStruct((1, groups), jnp.int32), [planes], weight=10**9)
    near, order = lax.optimization_barrier((near, order))
    cross = [
        lax.ppermute(jnp.where(odd, other_line, near), ("chan", "zp", "y"), turn_pairs(groups, ny, k))
        for k, other_line in enumerate(side, 1)
    ]

    lefts = [t] + side + [near]
    vm, w = call(
        first_kernel,
        [jax.ShapeDtypeStruct((width, width), BF16), jax.ShapeDtypeStruct((len(lefts) * rows, width), BF16)],
        [channel_dims[None, :], v] + lefts,
    )
    return call(
        functools.partial(tiles_kernel, half),
        jax.ShapeDtypeStruct((groups, 2 * ny, rows // 2, 2 * half), BF16),
        [order, owner_map[None, :], w, vm, near] + cross + shares,
        scratch=[pltpu.VMEM((groups * half, width), BF16)],
    )


def per_device(t_matrix, v_jacobi, channel_dims, owner_map):
    t, v = t_matrix[0], v_jacobi[0]
    rows = t.shape[0]
    half = rows // 2
    groups, ny = lax.axis_size("chan"), lax.axis_size("y")
    tiles = lab_tiles(t, v, channel_dims, owner_map)

    sent = tiles.reshape(groups * 2 * ny, rows // 2, 2 * half)
    got = lax.all_to_all(sent, ("chan", "zp", "y"), split_axis=0, concat_axis=0, tiled=True)
    got = got.reshape(groups, 2 * ny, rows // 2, 2 * half)
    out = call(
        functools.partial(place_kernel, ny, half),
        jax.ShapeDtypeStruct((groups, rows, ny * rows), BF16),
        [got],
        scratch=[pltpu.VMEM((groups, rows, ny * rows), BF16), pltpu.SemaphoreType.DMA((groups,))],
        out_space=pl.ANY,
    )
    return out[None]


def solution(mesh):
    chan, blk = mesh.shape["chan"], mesh.shape["blk"]

    def whole(t_matrix, v_jacobi, channel_dims, owner_map):
        block_cols = t_matrix.shape[1] // chan
        ny = block_cols * blk // t_matrix.shape[1]
        inner = Mesh(mesh.devices.reshape(chan, blk // (2 * ny), 2, ny), ("chan", "zg", "zp", "y"))
        line = ("zg", "zp", "y")
        return jax.shard_map(
            per_device,
            mesh=inner,
            in_specs=(P("chan", line, None), P("chan", None, None), P("chan"), P()),
            out_specs=P("chan", None, line, None),
            check_vma=False,
        )(t_matrix, v_jacobi, channel_dims, owner_map)

    return whole
```
